32 devices in a mesh: co: 16 (over z, y, core), ci: 2 (over x).
Axes of the slice: x: 2, y: 2, z: 4, core: 2. Of those that a mesh axis runs over, the one named last changes fastest.
Arguments:
- features: bfloat16 [1024, 1024], P('ci'), may hold values from -6 to 6
- filter_bank: bfloat16 [27, 1024, 1024], P(None, 'co', 'ci'), may hold values from -0.0390625 to 0.0390625
- out_grad: bfloat16 [1024, 1024], P('co', 'ci'), may hold values from -6 to 6
Outputs:
- response: bfloat16 [1024, 1024], P('co', 'ci')
- in_grad: bfloat16 [1024, 1024], P('ci', 'co')
- filter_grad: float32 [27, 1024, 1024], P(None, 'co', 'ci')
The draws below stay inside these ranges and needn't reach their ends.
All inputs are finite; a program needn't handle non-finite values.
Results may differ from the reference program's by a relative error of at most 0.001.
Values may be sent and summed in bfloat16 or wider, within the bound.
A program may use at most 64 MiB of HBM per device.

```python
import jax
import jax.numpy as jnp
from jax import lax

CIN = 1024
COUT = 1024
NY = 8
NZ = 8
NX = 16
TAPS = 27


def with_spikes(drawn, stream_key, source, target, blocks, factor):
    owner, partner = [(jnp.arange(drawn.shape[dim]) // (drawn.shape[dim] // blocks)).reshape([-1 if axis == dim else 1 for axis in range(drawn.ndim)]) for dim in (source, target)]
    chosen = jax.random.permutation(stream_key, blocks)[partner]
    strong = (owner == chosen) | (owner == (partner + blocks // 2) % blocks)
    return jnp.where(strong, factor * drawn, drawn)


def level_of(own_key, dims, split, smallest, top_value):
    def one(axis_at, parts):
        heights = jax.random.uniform(jax.random.fold_in(jax.random.fold_in(own_key, 6), axis_at), (parts,), jnp.float32, smallest / len(split), top_value / len(split))
        return jnp.repeat(jnp.exp(heights), dims[axis_at] // parts).reshape((-1,) + (1,) * (len(dims) - axis_at - 1))

    loudness = one(*split[0])
    for cut in split[1:]:
        loudness = loudness * one(*cut)
    return loudness


def noise(rng, dims, spread, bound, cuts=(), dtype=jnp.bfloat16):
    factor_of = level_of(rng, dims, cuts, -0.22, 0.18) if cuts else 1.0
    entries = jax.random.normal(rng, dims, jnp.float32) * spread * factor_of
    return jnp.minimum(jnp.maximum(entries, -bound), bound).astype(dtype)


def noise_with(key, extent, deviation, bound, cuts, heavy, held_as=jnp.bfloat16):
    drawn = deviation * jax.random.normal(key, extent, jnp.float32)
    if cuts:
        drawn = drawn * level_of(key, extent, cuts, -0.22, 0.18)
    return jnp.clip(with_spikes(drawn, jax.random.fold_in(key, 3), *heavy), -bound, bound).astype(held_as)


def setup_inputs(seed: int = 0) -> dict:
    keys = jax.random.split(jax.random.key(seed), 4)
    features = noise_with(keys[0], (CIN, NX * NY * NZ), 1.0, 6.0, ((0, 2),), (0, 1, 2, 2.0))
    filter_bank = noise(keys[1], (TAPS, COUT, CIN), (TAPS * CIN) ** -0.5, 0.0390625, ((1, 16), (2, 2)))
    out_grad = noise_with(keys[2], (COUT, NX * NY * NZ), 1.0, 6.0, ((0, 16), (1, 2)), (0, 1, 16, 2.0))
    return {"features": features, "filter_bank": filter_bank, "out_grad": out_grad}


def reference(features, filter_bank, out_grad):
    cell_count = NX * NY * NZ
    volume = features.astype(jnp.float32).reshape(1, CIN, NX, NY, NZ)
    kernel = filter_bank.astype(jnp.float32).reshape(3, 3, 3, COUT, CIN)
    pads = ((1, 1), (1, 1), (1, 1))
    response = lax.conv_general_dilated(volume, kernel, (1, 1, 1), pads, dimension_numbers=("NCDHW", "DHWOI", "NCDHW"), precision=lax.Precision.HIGHEST)
    response = response.reshape(COUT, cell_count).astype(jnp.bfloat16)
    gradient = out_grad.astype(jnp.float32)
    flipped = kernel[::-1, ::-1, ::-1]
    in_grad = lax.conv_general_dilated(gradient.reshape(1, COUT, NX, NY, NZ), flipped, (1, 1, 1), pads, dimension_numbers=("NCDHW", "DHWIO", "NCDHW"), precision=lax.Precision.HIGHEST)
    in_grad = in_grad.reshape(CIN, cell_count).astype(jnp.bfloat16)
    padded = jnp.pad(features.astype(jnp.float32).reshape(CIN, NX, NY, NZ), ((0, 0), (1, 1), (1, 1), (1, 1)))
    scale = float(cell_count) ** -0.5
    blocks = []
    for first in range(3):
        for second in range(3):
            for third in range(3):
                shifted = padded[:, first:first + NX, second:second + NY, third:third + NZ].reshape(CIN, cell_count)
                blocks.append(jnp.dot(gradient, shifted.T, precision=lax.Precision.HIGHEST) * scale)
    filter_grad = jnp.stack(blocks, axis=0)
    return response, in_grad, filter_grad
```

```python
import functools

import jax
import jax.numpy as jnp
from jax import lax
from jax.experimental import pallas as pl
from jax.experimental.pallas import tpu as pltpu
from jax.sharding import PartitionSpec as P

NY = 8
NZ = 8
PLANE = NY * NZ
LANES = 128
MESH = pl.DeviceIdType.MESH


def place(plane, order):
    spot = 0
    for bit in order:
        spot = spot * 2 + (plane >> bit) % 2
    return spot


def kernel(
    n_co, n_ci, orders,
    f_hbm, w_hbm, g_hbm,
    resp_ref, ingrad_ref, fg_hbm,
    f_ref, w_ref, g_ref, base, acc, recvs, ysum, rpart, rrecv, u_mid, u_side, fg_ref,
    in_sem, gs_sem, gr_sem, rs_sem, rr_sem, hs_sem, hr_sem, out_sem,
):
    cells = f_ref.shape[1]
    ci_n = f_ref.shape[0]
    co_n, half = g_ref.shape[1], g_ref.shape[2]
    planes = cells // PLANE
    rows_w = 27 * co_n
    depth = 3 * co_n
    wide = base.shape[2]
    stages = len(orders[0])
    chunks = len(orders)
    co_me = lax.axis_index("co")
    ci_me = lax.axis_index("ci")

    def co_bit(bit):
        return lax.rem(co_me // (1 << bit), 2)

    def co_partner(bit):
        return co_me + (1 - 2 * co_bit(bit)) * (1 << bit)

    def ci_other(d):
        return lax.rem(ci_me + d, n_ci)

    load_w = pltpu.make_async_copy(w_hbm, w_ref.at[pl.ds(0, rows_w)], in_sem.at[0])
    load_f = pltpu.make_async_copy(f_hbm, f_ref, in_sem.at[1])
    load_g = pltpu.make_async_copy(g_hbm, g_ref.at[ci_me], in_sem.at[2])
    load_w.start()
    load_f.start()
    load_g.start()

    barrier = pltpu.get_barrier_semaphore()
    for bit in range(stages):
        pl.semaphore_signal(barrier, inc=1, device_id={"co": co_partner(bit)}, device_id_type=MESH)
    for d in range(1, n_ci):
        pl.semaphore_signal(barrier, inc=1, device_id={"ci": ci_other(d)}, device_id_type=MESH)
    pl.semaphore_wait(barrier, stages + n_ci - 1)

    g_copies = []
    for d in range(1, n_ci):
        copy = pltpu.make_async_remote_copy(
            src_ref=g_hbm, dst_ref=g_ref.at[ci_me],
            send_sem=gs_sem.at[d - 1], recv_sem=gr_sem.at[d - 1],
            device_id={"ci": ci_other(d)}, device_id_type=MESH,
        )
        copy.start()
        g_copies.append(copy)

    w_ref[rows_w:, :] = jnp.zeros((w_ref.shape[0] - rows_w, ci_n), w_ref.dtype)
    base[:, 0:PLANE, :] = jnp.zeros((3, PLANE, wide), base.dtype)
    base[:, PLANE + cells:, :] = jnp.zeros((3, PLANE, wide), base.dtype)
    load_w.wait()
    load_f.wait()

    tile = 2 * LANES

    def response_tile(at):
        lane = lax.broadcasted_iota(jnp.int32, (co_n, tile), 1)
        k, j = lane & (NZ - 1), (lane // NZ) & (NY - 1)
        cols = f_ref[:, at * tile:(at + 1) * tile]
        for a in range(3):
            prod = jnp.dot(w_ref[a * 9 * co_n:(a + 1) * 9 * co_n, :], cols, preferred_element_type=jnp.float32)
            total = None
            for b in range(3):
                z = [prod[(3 * b + c) * co_n:(3 * b + c + 1) * co_n] for c in range(3)]
                part = z[1] + jnp.where(k > 0, pltpu.roll(z[0], 1, 1), 0.0)
                part = part + jnp.where(k < NZ - 1, pltpu.roll(z[2], tile - 1, 1), 0.0)
                if b == 0:
                    part = jnp.where(j > 0, pltpu.roll(part, NZ, 1), 0.0)
                if b == 2:
                    part = jnp.where(j < NY - 1, pltpu.roll(part, tile - NZ, 1), 0.0)
                total = part if total is None else total + part
            ysum[a, :, at * tile:(at + 1) * tile] = total

    tiles = cells // tile
    early = tiles // 2
    for at in range(early):
        response_tile(at)

    load_g.wait()
    for copy in g_copies:
        copy.wait_recv()
    grad = jnp.concatenate([g_ref[n] for n in range(n_ci)], axis=1).astype(jnp.float32)

    turned = jnp.concatenate([grad] * (wide // co_n), axis=0).T.reshape(cells // NZ, NZ, wide)
    lane = lax.broadcasted_iota(jnp.int32, turned.shape, 2)
    k = lax.broadcasted_iota(jnp.int32, turned.shape, 1)
    before = jnp.where(k < NZ - 1, pltpu.roll(turned, NZ - 1, 1), 0.0)
    after = jnp.where((k > 0) & (lane < 3 * co_n), pltpu.roll(turned, 1, 1), 0.0)
    mixed = jnp.where(lane < co_n, before, jnp.where(lane < 2 * co_n, turned, after))
    mixed = mixed.reshape(planes, NY, NZ, wide)
    blank = jnp.zeros((planes, 1, NZ, wide), jnp.float32)
    shifted = (
        jnp.concatenate([mixed[:, 1:], blank], axis=1),
        mixed,
        jnp.concatenate([blank, mixed[:, :-1]], axis=1),
    )
    for b in range(3):
        base[b, PLANE:PLANE + cells, :] = shifted[b].reshape(cells, wide).astype(base.dtype)

    cols_w = min(2 * LANES, ci_n)
    group = 8
    per = cols_w // LANES

    def shares(h):
        for first in range(0, planes, group):
            total = None
            for a in range(3):
                for b in range(3):
                    start = (first + 2 - a) * PLANE
                    top = (3 * a + b) * depth
                    term = jnp.dot(
                        base[b, start:start + group * PLANE, :],
                        w_ref[top:top + wide, h * cols_w:(h + 1) * cols_w],
                        preferred_element_type=jnp.float32,
                    )
                    total = term if total is None else total + term
            for q in range(per):
                c = h * per + q
                for p in range(group):
                    acc[c, place(first + p, orders[c])] = total[
                        p * PLANE:(p + 1) * PLANE, q * LANES:(q + 1) * LANES
                    ]

    def where_at(c, s):
        spot = 0
        for n in range(s):
            spot = spot + co_bit(orders[c][n]) * (n_co >> (n + 1))
        return spot

    def halving(c, s):
        size = n_co >> (s + 1)
        bit = orders[c][s]
        return pltpu.make_async_remote_copy(
            src_ref=acc.at[c, pl.ds(where_at(c, s) + (1 - co_bit(bit)) * size, size)],
            dst_ref=recvs[s].at[c],
            send_sem=hs_sem.at[c * stages + s], recv_sem=hr_sem.at[c * stages + s],
            device_id={"co": co_partner(bit)}, device_id_type=MESH,
        )

    def begin(c, s):
        halving(c, s).start()

    def step(c, s):
        halving(c, s).wait_recv()
        size = n_co >> (s + 1)
        spot = pl.ds(where_at(c, s + 1), size)
        if s + 1 < stages:
            acc[c, spot] = acc[c, spot] + recvs[s][c]
            begin(c, s + 1)
        else:
            block = acc[c, where_at(c, s + 1)] + recvs[s][c, 0]
            ingrad_ref[c * LANES:(c + 1) * LANES, :] = block.T.astype(ingrad_ref.dtype)

    halves = ci_n // cols_w
    for h in range(halves):
        shares(h)
        for q in range(per):
            begin(h * per + q, 0)
    for c in range(chunks // 2):
        step(c, 0)

    for at in range(early, tiles):
        response_tile(at)
    for c in range(chunks // 2, chunks):
        step(c, 0)

    lane = lax.broadcasted_iota(jnp.int32, (co_n, cells), 1)
    whole = ysum[1] + jnp.where(lane >= PLANE, pltpu.roll(ysum[0], PLANE, 1), 0.0)
    whole = whole + jnp.where(lane < cells - PLANE, pltpu.roll(ysum[2], cells - PLANE, 1), 0.0)
    for n in range(n_ci):
        rpart[n] = whole[:, n * half:(n + 1) * half]
    r_copies = []
    for d in range(1, n_ci):
        copy = pltpu.make_async_remote_copy(
            src_ref=rpart.at[ci_other(d)], dst_ref=rrecv.at[d - 1],
            send_sem=rs_sem.at[d - 1], recv_sem=rr_sem.at[d - 1],
            device_id={"ci": ci_other(d)}, device_id_type=MESH,
        )
        copy.start()
        r_copies.append(copy)

    k, j = lane & (NZ - 1), (lane // NZ) & (NY - 1)
    edge = jnp.zeros((co_n, LANES), jnp.float32)
    along = (
        jnp.where(k < NZ - 1, pltpu.roll(grad, cells - 1, 1), 0.0),
        grad,
        jnp.where(k > 0, pltpu.roll(grad, 1, 1), 0.0),
    )
    for b in range(3):
        for c in range(3):
            v = along[c]
            if b == 0:
                v = jnp.where(j < NY - 1, pltpu.roll(v, cells - NZ, 1), 0.0)
            if b == 2:
                v = jnp.where(j > 0, pltpu.roll(v, NZ, 1), 0.0)
            rows = slice((3 * b + c) * co_n, (3 * b + c + 1) * co_n)
            u_mid[rows, :] = v.astype(u_mid.dtype)
            u_side[rows, :] = pltpu.roll(jnp.concatenate([v, edge], axis=1), PLANE, 1).astype(u_side.dtype)

    scale = float(cells) ** -0.5
    out_copies = []

    def weights(a):
        left = u_mid[...] if a == 1 else (u_side[:, 2 * PLANE:2 * PLANE + cells] if a == 0 else u_side[:, 0:cells])
        prod = lax.dot_general(left, f_ref[...], (((1,), (1,)), ((), ())), preferred_element_type=jnp.float32)
        rows = pl.ds(a * 9 * co_n, 9 * co_n)
        fg_ref[rows, :] = prod * scale
        copy = pltpu.make_async_copy(fg_ref.at[rows], fg_hbm.at[rows], out_sem.at[a])
        copy.start()
        out_copies.append(copy)

    todo = [(c, s) for t in range(1, stages + chunks) for c in range(chunks) for s in [t - c] if 1 <= s < stages]
    at_todo = 0
    for a in range(3):
        for _ in range(2):
            if at_todo < len(todo):
                step(*todo[at_todo])
                at_todo += 1
        weights(a)
    for c, s in todo[at_todo:]:
        step(c, s)

    mine = rpart[ci_me]
    for d in range(1, n_ci):
        r_copies[d - 1].wait_recv()
        mine = mine + rrecv[d - 1]
    resp_ref[...] = mine.astype(resp_ref.dtype)

    for c in range(chunks):
        for s in range(stages):
            halving(c, s).wait_send()
    for copy in g_copies + r_copies:
        copy.wait_send()
    for copy in out_copies:
        copy.wait()


def body(n_co, n_ci, features, filter_bank, out_grad):
    ci_n, cells = features.shape
    co_n, half = out_grad.shape
    stages = n_co.bit_length() - 1
    chunks = ci_n // LANES
    near = tuple(range(stages))
    far = (0,) + tuple(range(2, stages)) + (1,)
    orders = tuple(far if c == 1 else near for c in range(chunks))
    wide = -(-3 * co_n // LANES) * LANES
    rows_w = 27 * co_n
    dma = pltpu.SemaphoreType.DMA
    other = max(n_ci - 1, 1)
    scratch = [
        pltpu.VMEM((ci_n, cells), jnp.bfloat16),
        pltpu.VMEM((rows_w + wide - 3 * co_n, ci_n), jnp.bfloat16),
        pltpu.VMEM((n_ci, co_n, half), jnp.bfloat16),
        pltpu.VMEM((3, cells + 2 * PLANE, wide), jnp.bfloat16),
        pltpu.VMEM((chunks, n_co, PLANE, LANES), jnp.float32),
        [pltpu.VMEM((chunks, n_co >> (s + 1), PLANE, LANES), jnp.float32) for s in range(stages)],
        pltpu.VMEM((3, co_n, cells), jnp.float32),
        pltpu.VMEM((n_ci, co_n, half), jnp.float32),
        pltpu.VMEM((other, co_n, half), jnp.float32),
        pltpu.VMEM((9 * co_n, cells), jnp.bfloat16),
        pltpu.VMEM((9 * co_n, cells + 2 * PLANE), jnp.bfloat16),
        pltpu.VMEM((rows_w, ci_n), jnp.float32),
        dma((3,)), dma((other,)), dma((other,)), dma((other,)), dma((other,)),
        dma((chunks * stages,)), dma((chunks * stages,)), dma((3,)),
    ]
    anywhere = pl.BlockSpec(memory_space=pl.ANY)
    vmem = pl.BlockSpec(memory_space=pltpu.VMEM)
    response, in_grad, filter_grad = pl.pallas_call(
        functools.partial(kernel, n_co, n_ci, orders),
        out_shape=(
            jax.ShapeDtypeStruct((co_n, half), jnp.bfloat16),
            jax.ShapeDtypeStruct((ci_n, cells // n_co), jnp.bfloat16),
            jax.ShapeDtypeStruct((rows_w, ci_n), jnp.float32),
        ),
        in_specs=[anywhere] * 3,
        out_specs=(vmem, vmem, anywhere),
        scratch_shapes=scratch,
        compiler_params=pltpu.CompilerParams(
            collective_id=0, has_side_effects=True, vmem_limit_bytes=48 * 1024 * 1024
        ),
        cost_estimate=pl.CostEstimate(
            flops=6 * rows_w * ci_n * cells, bytes_accessed=8 * rows_w * ci_n, transcendentals=0
        ),
    )(features, filter_bank.reshape(rows_w, ci_n), out_grad)
    return response, in_grad, filter_grad.reshape(27, co_n, ci_n)


def solution(mesh):
    placed = (P("ci", None), P(None, "co", "ci"), P("co", "ci"))
    return jax.shard_map(
        functools.partial(body, mesh.shape["co"], mesh.shape["ci"]),
        mesh=mesh,
        in_specs=placed,
        out_specs=(P("co", "ci"), P("ci", "co"), P(None, "co", "ci")),
        check_vma=False,
    )
```

```python
import functools

import jax
import jax.numpy as jnp
from jax import lax
from jax.experimental import pallas as pl
from jax.experimental.pallas import tpu as pltpu
from jax.sharding import PartitionSpec as P

NY = 8
NZ = 8
PLANE = NY * NZ
LANES = 128
MESH = pl.DeviceIdType.MESH


def place(plane, order):
    spot = 0
    for bit in order:
        spot = spot * 2 + (plane >> bit) % 2
    return spot


def kernel(
    n_co, n_ci, orders,
    f_hbm, w_hbm, g_hbm,
    resp_ref, ingrad_ref, fg_ref,
    f_ref, w_ref, g_ref, base, acc, recvs, ysum, rpart, rrecv, u_mid, u_side,
    in_sem, gs_sem, gr_sem, rs_sem, rr_sem, hs_sem, hr_sem,
):
    cells = f_ref.shape[1]
    ci_n = f_ref.shape[0]
    co_n, half = g_ref.shape[1], g_ref.shape[2]
    planes = cells // PLANE
    rows_w = 27 * co_n
    depth = 3 * co_n
    wide = base.shape[2]
    stages = len(orders[0])
    chunks = len(orders)
    co_me = lax.axis_index("co")
    ci_me = lax.axis_index("ci")

    def co_bit(bit):
        return lax.rem(co_me // (1 << bit), 2)

    def co_partner(bit):
        return co_me + (1 - 2 * co_bit(bit)) * (1 << bit)

    def ci_other(d):
        return lax.rem(ci_me + d, n_ci)

    load_w = pltpu.make_async_copy(w_hbm, w_ref.at[pl.ds(0, rows_w)], in_sem.at[0])
    load_f = pltpu.make_async_copy(f_hbm, f_ref, in_sem.at[1])
    load_g = pltpu.make_async_copy(g_hbm, g_ref.at[ci_me], in_sem.at[2])
    load_w.start()
    load_f.start()
    load_g.start()

    barrier = pltpu.get_barrier_semaphore()
    for bit in range(stages):
        pl.semaphore_signal(barrier, inc=1, device_id={"co": co_partner(bit)}, device_id_type=MESH)
    for d in range(1, n_ci):
        pl.semaphore_signal(barrier, inc=1, device_id={"ci": ci_other(d)}, device_id_type=MESH)
    pl.semaphore_wait(barrier, stages + n_ci - 1)

    g_copies = []
    for d in range(1, n_ci):
        copy = pltpu.make_async_remote_copy(
            src_ref=g_hbm, dst_ref=g_ref.at[ci_me],
            send_sem=gs_sem.at[d - 1], recv_sem=gr_sem.at[d - 1],
            device_id={"ci": ci_other(d)}, device_id_type=MESH,
        )
        copy.start()
        g_copies.append(copy)

    w_ref[rows_w:, :] = jnp.zeros((w_ref.shape[0] - rows_w, ci_n), w_ref.dtype)
    base[:, 0:PLANE, :] = jnp.zeros((3, PLANE, wide), base.dtype)
    base[:, PLANE + cells:, :] = jnp.zeros((3, PLANE, wide), base.dtype)
    load_w.wait()
    load_f.wait()

    tile = 2 * LANES

    def response_tile(at):
        lane = lax.broadcasted_iota(jnp.int32, (co_n, tile), 1)
        k, j = lane & (NZ - 1), (lane // NZ) & (NY - 1)
        cols = f_ref[:, at * tile:(at + 1) * tile]
        for a in range(3):
            prod = jnp.dot(w_ref[a * 9 * co_n:(a + 1) * 9 * co_n, :], cols, preferred_element_type=jnp.float32)
            total = None
            for b in range(3):
                z = [prod[(3 * b + c) * co_n:(3 * b + c + 1) * co_n] for c in range(3)]
                part = z[1] + jnp.where(k > 0, pltpu.roll(z[0], 1, 1), 0.0)
                part = part + jnp.where(k < NZ - 1, pltpu.roll(z[2], tile - 1, 1), 0.0)
                if b == 0:
                    part = jnp.where(j > 0, pltpu.roll(part, NZ, 1), 0.0)
                if b == 2:
                    part = jnp.where(j < NY - 1, pltpu.roll(part, tile - NZ, 1), 0.0)
                total = part if total is None else total + part
            ysum[a, :, at * tile:(at + 1) * tile] = total

    tiles = cells // tile
    early = tiles // 2
    for at in range(early):
        response_tile(at)

    load_g.wait()
    for copy in g_copies:
        copy.wait_recv()
    grad = jnp.concatenate([g_ref[n] for n in range(n_ci)], axis=1).astype(jnp.float32)

    turned = jnp.concatenate([grad] * (wide // co_n), axis=0).T.reshape(cells // NZ, NZ, wide)
    lane = lax.broadcasted_iota(jnp.int32, turned.shape, 2)
    k = lax.broadcasted_iota(jnp.int32, turned.shape, 1)
    before = jnp.where(k < NZ - 1, pltpu.roll(turned, NZ - 1, 1), 0.0)
    after = jnp.where((k > 0) & (lane < 3 * co_n), pltpu.roll(turned, 1, 1), 0.0)
    mixed = jnp.where(lane < co_n, before, jnp.where(lane < 2 * co_n, turned, after))
    mixed = mixed.reshape(planes, NY, NZ, wide)
    blank = jnp.zeros((planes, 1, NZ, wide), jnp.float32)
    shifted = (
        jnp.concatenate([mixed[:, 1:], blank], axis=1),
        mixed,
        jnp.concatenate([blank, mixed[:, :-1]], axis=1),
    )
    for b in range(3):
        base[b, PLANE:PLANE + cells, :] = shifted[b].reshape(cells, wide).astype(base.dtype)

    cols_w = min(2 * LANES, ci_n)
    group = 8
    per = cols_w // LANES

    def shares(h):
        for first in range(0, planes, group):
            total = None
            for a in range(3):
                for b in range(3):
                    start = (first + 2 - a) * PLANE
                    top = (3 * a + b) * depth
                    term = jnp.dot(
                        base[b, start:start + group * PLANE, :],
                        w_ref[top:top + wide, h * cols_w:(h + 1) * cols_w],
                        preferred_element_type=jnp.float32,
                    )
                    total = term if total is None else total + term
            for q in range(per):
                c = h * per + q
                for p in range(group):
                    acc[c, place(first + p, orders[c])] = total[
                        p * PLANE:(p + 1) * PLANE, q * LANES:(q + 1) * LANES
                    ]

    def where_at(c, s):
        spot = 0
        for n in range(s):
            spot = spot + co_bit(orders[c][n]) * (n_co >> (n + 1))
        return spot

    def halving(c, s):
        size = n_co >> (s + 1)
        bit = orders[c][s]
        return pltpu.make_async_remote_copy(
            src_ref=acc.at[c, pl.ds(where_at(c, s) + (1 - co_bit(bit)) * size, size)],
            dst_ref=recvs[s].at[c],
            send_sem=hs_sem.at[c * stages + s], recv_sem=hr_sem.at[c * stages + s],
            device_id={"co": co_partner(bit)}, device_id_type=MESH,
        )

    def begin(c, s):
        halving(c, s).start()

    def step(c, s):
        halving(c, s).wait_recv()
        size = n_co >> (s + 1)
        spot = pl.ds(where_at(c, s + 1), size)
        if s + 1 < stages:
            acc[c, spot] = acc[c, spot] + recvs[s][c]
            begin(c, s + 1)
        else:
            block = acc[c, where_at(c, s + 1)] + recvs[s][c, 0]
            ingrad_ref[:, c * LANES:(c + 1) * LANES] = block.astype(ingrad_ref.dtype)

    halves = ci_n // cols_w
    for h in range(halves):
        shares(h)
        for q in range(per):
            begin(h * per + q, 0)
    for c in range(chunks // 2):
        step(c, 0)
    response_tile(early)
    for c in range(chunks // 2, chunks):
        step(c, 0)
    for at in range(early + 1, tiles):
        response_tile(at)

    lane = lax.broadcasted_iota(jnp.int32, (co_n, cells), 1)
    whole = ysum[1] + jnp.where(lane >= PLANE, pltpu.roll(ysum[0], PLANE, 1), 0.0)
    whole = whole + jnp.where(lane < cells - PLANE, pltpu.roll(ysum[2], cells - PLANE, 1), 0.0)
    for n in range(n_ci):
        rpart[n] = whole[:, n * half:(n + 1) * half]
    r_copies = []
    for d in range(1, n_ci):
        copy = pltpu.make_async_remote_copy(
            src_ref=rpart.at[ci_other(d)], dst_ref=rrecv.at[d - 1],
            send_sem=rs_sem.at[d - 1], recv_sem=rr_sem.at[d - 1],
            device_id={"ci": ci_other(d)}, device_id_type=MESH,
        )
        copy.start()
        r_copies.append(copy)

    todo = [(t - s, s) for t in range(1, stages + chunks) for s in range(stages - 1, 0, -1) if 0 <= t - s < chunks]

    def steps(count):
        for _ in range(min(count, len(todo))):
            step(*todo.pop(0))

    steps(1)
    k, j = lane & (NZ - 1), (lane // NZ) & (NY - 1)
    edge = jnp.zeros((co_n, LANES), jnp.float32)
    along = (
        jnp.where(k < NZ - 1, pltpu.roll(grad, cells - 1, 1), 0.0),
        grad,
        jnp.where(k > 0, pltpu.roll(grad, 1, 1), 0.0),
    )
    for b in range(3):
        for c in range(3):
            v = along[c]
            if b == 0:
                v = jnp.where(j < NY - 1, pltpu.roll(v, cells - NZ, 1), 0.0)
            if b == 2:
                v = jnp.where(j > 0, pltpu.roll(v, NZ, 1), 0.0)
            rows = slice((3 * b + c) * co_n, (3 * b + c + 1) * co_n)
            u_mid[rows, :] = v.astype(u_mid.dtype)
            u_side[rows, :] = pltpu.roll(jnp.concatenate([v, edge], axis=1), PLANE, 1).astype(u_side.dtype)


    scale = float(cells) ** -0.5

    def weights(a):
        left = u_mid[...] if a == 1 else (u_side[:, 2 * PLANE:2 * PLANE + cells] if a == 0 else u_side[:, 0:cells])
        prod = lax.dot_general(left, f_ref[...], (((1,), (1,)), ((), ())), preferred_element_type=jnp.float32)
        fg_ref[a * 9 * co_n:(a + 1) * 9 * co_n, :] = prod * scale

    steps(2)
    weights(1)
    steps(3)
    weights(0)
    steps(3)
    weights(2)
    steps(len(todo))

    mine = rpart[ci_me]
    for d in range(1, n_ci):
        r_copies[d - 1].wait_recv()
        mine = mine + rrecv[d - 1]
    resp_ref[...] = mine.astype(resp_ref.dtype)

    for c in range(chunks):
        for s in range(stages):
            halving(c, s).wait_send()
    for copy in g_copies + r_copies:
        copy.wait_send()


def hand_over(r_ref, i_ref, w_ref, r_out, i_out, w_out, sem):
    rows = w_ref.shape[0] // 3
    copies = [pltpu.make_async_copy(r_ref, r_out, sem.at[0]), pltpu.make_async_copy(i_ref, i_out, sem.at[1])]
    for a in range(3):
        part = pl.ds(a * rows, rows)
        copies.append(pltpu.make_async_copy(w_ref.at[part], w_out.at[part], sem.at[2 + a]))
    for copy in copies:
        copy.start()
    for copy in copies:
        copy.wait()


def body(n_co, n_ci, features, filter_bank, out_grad):
    ci_n, cells = features.shape
    co_n, half = out_grad.shape
    stages = n_co.bit_length() - 1
    chunks = ci_n // LANES
    near = tuple(range(stages))
    far = (0,) + tuple(range(2, stages)) + (1,)
    orders = tuple(far if c == 1 else near for c in range(chunks))
    wide = -(-3 * co_n // LANES) * LANES
    rows_w = 27 * co_n
    dma = pltpu.SemaphoreType.DMA
    other = max(n_ci - 1, 1)
    scratch = [
        pltpu.VMEM((ci_n, cells), jnp.bfloat16),
        pltpu.VMEM((rows_w + wide - 3 * co_n, ci_n), jnp.bfloat16),
        pltpu.VMEM((n_ci, co_n, half), jnp.bfloat16),
        pltpu.VMEM((3, cells + 2 * PLANE, wide), jnp.bfloat16),
        pltpu.VMEM((chunks, n_co, PLANE, LANES), jnp.float32),
        [pltpu.VMEM((chunks, n_co >> (s + 1), PLANE, LANES), jnp.float32) for s in range(stages)],
        pltpu.VMEM((3, co_n, cells), jnp.float32),
        pltpu.VMEM((n_ci, co_n, half), jnp.float32),
        pltpu.VMEM((other, co_n, half), jnp.float32),
        pltpu.VMEM((9 * co_n, cells), jnp.bfloat16),
        pltpu.VMEM((9 * co_n, cells + 2 * PLANE), jnp.bfloat16),
        dma((3,)), dma((other,)), dma((other,)), dma((other,)), dma((other,)),
        dma((chunks * stages,)), dma((chunks * stages,)),
    ]
    hbm = pl.BlockSpec(memory_space=pltpu.HBM)
    vmem = pl.BlockSpec(memory_space=pltpu.VMEM)
    shapes = (
        jax.ShapeDtypeStruct((co_n, half), jnp.bfloat16),
        jax.ShapeDtypeStruct((cells // n_co, ci_n), jnp.bfloat16),
        jax.ShapeDtypeStruct((rows_w, ci_n), jnp.float32),
    )
    results = pl.pallas_call(
        functools.partial(kernel, n_co, n_ci, orders),
        out_shape=shapes,
        in_specs=[hbm] * 3,
        out_specs=(vmem,) * 3,
        scratch_shapes=scratch,
        compiler_params=pltpu.CompilerParams(
            collective_id=0, has_side_effects=True, vmem_limit_bytes=32 * 1024 * 1024
        ),
        cost_estimate=pl.CostEstimate(
            flops=6 * rows_w * ci_n * cells, bytes_accessed=8 * rows_w * ci_n, transcendentals=0
        ),
    )(*[pltpu.with_memory_space_constraint(v, pltpu.HBM) for v in (features, filter_bank.reshape(rows_w, ci_n), out_grad)])
    response, in_grad, filter_grad = pl.pallas_call(
        hand_over,
        out_shape=shapes,
        in_specs=[vmem] * 3,
        out_specs=(hbm,) * 3,
        scratch_shapes=[dma((5,))],
        cost_estimate=pl.CostEstimate(flops=0, bytes_accessed=8 * rows_w * ci_n, transcendentals=0),
    )(*results)
    return response, in_grad.T, filter_grad.reshape(27, co_n, ci_n)


def solution(mesh):
    placed = (P("ci", None), P(None, "co", "ci"), P("co", "ci"))
    return jax.shard_map(
        functools.partial(body, mesh.shape["co"], mesh.shape["ci"]),
        mesh=mesh,
        in_specs=placed,
        out_specs=(P("co", "ci"), P("ci", "co"), P(None, "co", "ci")),
        check_vma=False,
    )
```

```python
import functools

import jax
import jax.numpy as jnp
from jax import lax
from jax.experimental import pallas as pl
from jax.experimental.pallas import tpu as pltpu
from jax.sharding import PartitionSpec as P

NY = 8
NZ = 8
PLANE = NY * NZ
LANES = 128
MESH = pl.DeviceIdType.MESH


def place(plane, order):
    spot = 0
    for bit in order:
        spot = spot * 2 + (plane >> bit) % 2
    return spot


def kernel(
    n_co, n_ci, orders,
    f_hbm, w_hbm, g_hbm,
    resp_ref, ingrad_ref, fg_ref,
    f_ref, w_ref, g_ref, base, acc, recvs, ysum, rpart, rrecv, u_mid, u_side,
    in_sem, gs_sem, gr_sem, rs_sem, rr_sem, hs_sem, hr_sem,
):
    cells = f_ref.shape[1]
    ci_n = f_ref.shape[0]
    co_n, half = g_ref.shape[1], g_ref.shape[2]
    planes = cells // PLANE
    rows_w = 27 * co_n
    depth = 3 * co_n
    wide = base.shape[2]
    stages = len(orders[0])
    chunks = len(orders)
    co_me = lax.axis_index("co")
    ci_me = lax.axis_index("ci")

    def co_bit(bit):
        return lax.rem(co_me // (1 << bit), 2)

    def co_partner(bit):
        return co_me + (1 - 2 * co_bit(bit)) * (1 << bit)

    def ci_other(d):
        return lax.rem(ci_me + d, n_ci)

    load_w = pltpu.make_async_copy(w_hbm, w_ref.at[pl.ds(0, rows_w)], in_sem.at[0])
    load_f = pltpu.make_async_copy(f_hbm, f_ref, in_sem.at[1])
    load_g = pltpu.make_async_copy(g_hbm, g_ref.at[ci_me], in_sem.at[2])
    load_w.start()
    load_f.start()
    load_g.start()

    barrier = pltpu.get_barrier_semaphore()
    for bit in range(stages):
        pl.semaphore_signal(barrier, inc=1, device_id={"co": co_partner(bit)}, device_id_type=MESH)
    for d in range(1, n_ci):
        pl.semaphore_signal(barrier, inc=1, device_id={"ci": ci_other(d)}, device_id_type=MESH)
    pl.semaphore_wait(barrier, stages + n_ci - 1)

    g_copies = []
    for d in range(1, n_ci):
        copy = pltpu.make_async_remote_copy(
            src_ref=g_hbm, dst_ref=g_ref.at[ci_me],
            send_sem=gs_sem.at[d - 1], recv_sem=gr_sem.at[d - 1],
            device_id={"ci": ci_other(d)}, device_id_type=MESH,
        )
        copy.start()
        g_copies.append(copy)

    w_ref[rows_w:, :] = jnp.zeros((w_ref.shape[0] - rows_w, ci_n), w_ref.dtype)
    base[:, 0:PLANE, :] = jnp.zeros((3, PLANE, wide), base.dtype)
    base[:, PLANE + cells:, :] = jnp.zeros((3, PLANE, wide), base.dtype)
    load_w.wait()
    load_f.wait()

    tile = 2 * LANES

    def response_tile(at):
        lane = lax.broadcasted_iota(jnp.int32, (co_n, tile), 1)
        k, j = lane & (NZ - 1), (lane // NZ) & (NY - 1)
        cols = f_ref[:, at * tile:(at + 1) * tile]
        for a in range(3):
            prod = jnp.dot(w_ref[a * 9 * co_n:(a + 1) * 9 * co_n, :], cols, preferred_element_type=jnp.float32)
            total = None
            for b in range(3):
                z = [prod[(3 * b + c) * co_n:(3 * b + c + 1) * co_n] for c in range(3)]
                part = z[1] + jnp.where(k > 0, pltpu.roll(z[0], 1, 1), 0.0)
                part = part + jnp.where(k < NZ - 1, pltpu.roll(z[2], tile - 1, 1), 0.0)
                if b == 0:
                    part = jnp.where(j > 0, pltpu.roll(part, NZ, 1), 0.0)
                if b == 2:
                    part = jnp.where(j < NY - 1, pltpu.roll(part, tile - NZ, 1), 0.0)
                total = part if total is None else total + part
            ysum[a, :, at * tile:(at + 1) * tile] = total

    tiles = cells // tile
    early = tiles // 2
    for at in range(early):
        response_tile(at)

    load_g.wait()
    for copy in g_copies:
        copy.wait_recv()
    grad = jnp.concatenate([g_ref[n] for n in range(n_ci)], axis=1).astype(jnp.float32)

    turned = jnp.concatenate([grad] * (wide // co_n), axis=0).T.reshape(cells // NZ, NZ, wide)
    lane = lax.broadcasted_iota(jnp.int32, turned.shape, 2)
    k = lax.broadcasted_iota(jnp.int32, turned.shape, 1)
    before = jnp.where(k < NZ - 1, pltpu.roll(turned, NZ - 1, 1), 0.0)
    after = jnp.where((k > 0) & (lane < 3 * co_n), pltpu.roll(turned, 1, 1), 0.0)
    mixed = jnp.where(lane < co_n, before, jnp.where(lane < 2 * co_n, turned, after))
    mixed = mixed.reshape(planes, NY, NZ, wide)
    blank = jnp.zeros((planes, 1, NZ, wide), jnp.float32)
    shifted = (
        jnp.concatenate([mixed[:, 1:], blank], axis=1),
        mixed,
        jnp.concatenate([blank, mixed[:, :-1]], axis=1),
    )
    for b in range(3):
        base[b, PLANE:PLANE + cells, :] = shifted[b].reshape(cells, wide).astype(base.dtype)

    cols_w = min(2 * LANES, ci_n)
    group = 8
    per = cols_w // LANES

    def shares(h):
        for first in range(0, planes, group):
            total = None
            for a in range(3):
                for b in range(3):
                    start = (first + 2 - a) * PLANE
                    top = (3 * a + b) * depth
                    term = jnp.dot(
                        base[b, start:start + group * PLANE, :],
                        w_ref[top:top + wide, h * cols_w:(h + 1) * cols_w],
                        preferred_element_type=jnp.float32,
                    )
                    total = term if total is None else total + term
            for q in range(per):
                c = h * per + q
                for p in range(group):
                    acc[c, place(first + p, orders[c])] = total[
                        p * PLANE:(p + 1) * PLANE, q * LANES:(q + 1) * LANES
                    ]

    def where_at(c, s):
        spot = 0
        for n in range(s):
            spot = spot + co_bit(orders[c][n]) * (n_co >> (n + 1))
        return spot

    def halving(c, s):
        size = n_co >> (s + 1)
        bit = orders[c][s]
        return pltpu.make_async_remote_copy(
            src_ref=acc.at[c, pl.ds(where_at(c, s) + (1 - co_bit(bit)) * size, size)],
            dst_ref=recvs[s].at[c],
            send_sem=hs_sem.at[c * stages + s], recv_sem=hr_sem.at[c * stages + s],
            device_id={"co": co_partner(bit)}, device_id_type=MESH,
        )

    def begin(c, s):
        halving(c, s).start()

    def arrive(c, s):
        halving(c, s).wait_recv()
        size = n_co >> (s + 1)
        spot = pl.ds(where_at(c, s + 1), size)
        if s + 1 < stages:
            acc[c, spot] = acc[c, spot] + recvs[s][c]
        else:
            block = acc[c, where_at(c, s + 1)] + recvs[s][c, 0]
            ingrad_ref[:, c * LANES:(c + 1) * LANES] = block.astype(ingrad_ref.dtype)

    def step(c, s):
        arrive(c, s)
        if s + 1 < stages:
            begin(c, s + 1)

    halves = ci_n // cols_w
    for h in range(halves):
        shares(h)
        for q in range(per):
            begin(h * per + q, 0)
    lead = [0] + list(range(2, chunks))
    step(0, 0)
    if chunks > 1:
        step(1, 0)
    for at in range(early, tiles):
        response_tile(at)
    for c in lead[1:]:
        arrive(c, 0)

    lane = lax.broadcasted_iota(jnp.int32, (co_n, cells), 1)
    whole = ysum[1] + jnp.where(lane >= PLANE, pltpu.roll(ysum[0], PLANE, 1), 0.0)
    whole = whole + jnp.where(lane < cells - PLANE, pltpu.roll(ysum[2], cells - PLANE, 1), 0.0)
    for n in range(n_ci):
        rpart[n] = whole[:, n * half:(n + 1) * half]
    r_copies = []
    for d in range(1, n_ci):
        copy = pltpu.make_async_remote_copy(
            src_ref=rpart.at[ci_other(d)], dst_ref=rrecv.at[d - 1],
            send_sem=rs_sem.at[d - 1], recv_sem=rr_sem.at[d - 1],
            device_id={"ci": ci_other(d)}, device_id_type=MESH,
        )
        copy.start()
        r_copies.append(copy)

    k, j = lane & (NZ - 1), (lane // NZ) & (NY - 1)
    edge = jnp.zeros((co_n, LANES), jnp.float32)
    along = (
        jnp.where(k < NZ - 1, pltpu.roll(grad, cells - 1, 1), 0.0),
        grad,
        jnp.where(k > 0, pltpu.roll(grad, 1, 1), 0.0),
    )

    def lay(b):
        for c in range(3):
            v = along[c]
            if b == 0:
                v = jnp.where(j < NY - 1, pltpu.roll(v, cells - NZ, 1), 0.0)
            if b == 2:
                v = jnp.where(j > 0, pltpu.roll(v, NZ, 1), 0.0)
            rows = slice((3 * b + c) * co_n, (3 * b + c + 1) * co_n)
            u_mid[rows, :] = v.astype(u_mid.dtype)
            u_side[rows, :] = pltpu.roll(jnp.concatenate([v, edge], axis=1), PLANE, 1).astype(u_side.dtype)

    scale = float(cells) ** -0.5

    def weights(a, h):
        left = u_mid[...] if a == 1 else (u_side[:, 2 * PLANE:2 * PLANE + cells] if a == 0 else u_side[:, 0:cells])
        cols = slice(h * cols_w, (h + 1) * cols_w)
        prod = lax.dot_general(left, f_ref[cols, :], (((1,), (1,)), ((), ())), preferred_element_type=jnp.float32)
        fg_ref[a * 9 * co_n:(a + 1) * 9 * co_n, cols] = prod * scale

    work = [functools.partial(lay, b) for b in range(3)]
    work += [functools.partial(weights, a, h) for a in range(3) for h in range(halves)]

    def compute(count):
        for _ in range(min(count, len(work))):
            work.pop(0)()

    compute(1)
    open_at = {1: 1} if chunks > 1 else {}
    for turn, c in enumerate(lead):
        step(c, 1)
        if turn + 1 < len(lead):
            begin(lead[turn + 1], 1)
        for other in list(open_at):
            if open_at[other] < stages:
                step(other, open_at[other])
                open_at[other] += 1
            compute(1)
        open_at[c] = 2
        compute(1)
    while any(s < stages for s in open_at.values()):
        for other in open_at:
            if open_at[other] < stages:
                step(other, open_at[other])
                open_at[other] += 1
                compute(1)
    compute(len(work))

    mine = rpart[ci_me]
    for d in range(1, n_ci):
        r_copies[d - 1].wait_recv()
        mine = mine + rrecv[d - 1]
    resp_ref[...] = mine.astype(resp_ref.dtype)

    for c in range(chunks):
        for s in range(stages):
            halving(c, s).wait_send()
    for copy in g_copies + r_copies:
        copy.wait_send()


def hand_over(r_ref, i_ref, w_ref, r_out, i_out, w_out, sem):
    rows = w_ref.shape[0] // 27
    copies = [pltpu.make_async_copy(r_ref, r_out, sem.at[0]), pltpu.make_async_copy(i_ref, i_out, sem.at[1])]
    for t in range(27):
        part = pl.ds(t * rows, rows)
        copies.append(pltpu.make_async_copy(w_ref.at[part], w_out.at[part], sem.at[2 + t]))
    for copy in copies:
        copy.start()
    for copy in copies:
        copy.wait()


def body(n_co, n_ci, features, filter_bank, out_grad):
    ci_n, cells = features.shape
    co_n, half = out_grad.shape
    stages = n_co.bit_length() - 1
    chunks = ci_n // LANES
    near = tuple(range(stages))
    far = (0,) + tuple(range(2, stages)) + (1,)
    orders = tuple(far if c == 1 else near for c in range(chunks))
    wide = -(-3 * co_n // LANES) * LANES
    rows_w = 27 * co_n
    dma = pltpu.SemaphoreType.DMA
    other = max(n_ci - 1, 1)
    scratch = [
        pltpu.VMEM((ci_n, cells), jnp.bfloat16),
        pltpu.VMEM((rows_w + wide - 3 * co_n, ci_n), jnp.bfloat16),
        pltpu.VMEM((n_ci, co_n, half), jnp.bfloat16),
        pltpu.VMEM((3, cells + 2 * PLANE, wide), jnp.bfloat16),
        pltpu.VMEM((chunks, n_co, PLANE, LANES), jnp.float32),
        [pltpu.VMEM((chunks, n_co >> (s + 1), PLANE, LANES), jnp.float32) for s in range(stages)],
        pltpu.VMEM((3, co_n, cells), jnp.float32),
        pltpu.VMEM((n_ci, co_n, half), jnp.float32),
        pltpu.VMEM((other, co_n, half), jnp.float32),
        pltpu.VMEM((9 * co_n, cells), jnp.bfloat16),
        pltpu.VMEM((9 * co_n, cells + 2 * PLANE), jnp.bfloat16),
        dma((3,)), dma((other,)), dma((other,)), dma((other,)), dma((other,)),
        dma((chunks * stages,)), dma((chunks * stages,)),
    ]
    hbm = pl.BlockSpec(memory_space=pltpu.HBM)
    vmem = pl.BlockSpec(memory_space=pltpu.VMEM)
    shapes = (
        jax.ShapeDtypeStruct((co_n, half), jnp.bfloat16),
        jax.ShapeDtypeStruct((cells // n_co, ci_n), jnp.bfloat16),
        jax.ShapeDtypeStruct((rows_w, ci_n), jnp.float32),
    )
    results = pl.pallas_call(
        functools.partial(kernel, n_co, n_ci, orders),
        out_shape=shapes,
        in_specs=[hbm] * 3,
        out_specs=(vmem,) * 3,
        scratch_shapes=scratch,
        compiler_params=pltpu.CompilerParams(
            collective_id=0, has_side_effects=True, vmem_limit_bytes=32 * 1024 * 1024
        ),
        cost_estimate=pl.CostEstimate(
            flops=6 * rows_w * ci_n * cells, bytes_accessed=8 * rows_w * ci_n, transcendentals=0
        ),
    )(*[pltpu.with_memory_space_constraint(v, pltpu.HBM) for v in (features, filter_bank.reshape(rows_w, ci_n), out_grad)])
    response, in_grad, filter_grad = pl.pallas_call(
        hand_over,
        out_shape=shapes,
        in_specs=[vmem] * 3,
        out_specs=(hbm,) * 3,
        scratch_shapes=[dma((29,))],
        compiler_params=pltpu.CompilerParams(vmem_limit_bytes=8 * 1024 * 1024),
        cost_estimate=pl.CostEstimate(flops=0, bytes_accessed=8 * rows_w * ci_n, transcendentals=0),
    )(*[pltpu.with_memory_space_constraint(v, pltpu.VMEM) for v in results])
    return response, in_grad.T, filter_grad.reshape(27, co_n, ci_n)


def solution(mesh):
    placed = (P("ci", None), P(None, "co", "ci"), P("co", "ci"))
    return jax.shard_map(
        functools.partial(body, mesh.shape["co"], mesh.shape["ci"]),
        mesh=mesh,
        in_specs=placed,
        out_specs=(P("co", "ci"), P("ci", "co"), P(None, "co", "ci")),
        check_vma=False,
    )
```

```python
import functools

import jax
import jax.numpy as jnp
from jax import lax
from jax.experimental import pallas as pl
from jax.experimental.pallas import tpu as pltpu
from jax.sharding import PartitionSpec as P

NY = 8
NZ = 8
PLANE = NY * NZ
LANES = 128
MESH = pl.DeviceIdType.MESH


def place(plane, order):
    spot = 0
    for bit in order:
        spot = spot * 2 + (plane >> bit) % 2
    return spot


def kernel(
    n_co, n_ci, orders,
    f_hbm, w_hbm, g_hbm,
    resp_ref, ingrad_ref, fg_ref,
    f_ref, w_ref, g_ref, base, acc, recvs, ysum, rpart, rrecv, u_mid, u_side,
    in_sem, gs_sem, gr_sem, rs_sem, rr_sem, hs_sem, hr_sem,
):
    cells = f_ref.shape[1]
    ci_n = f_ref.shape[0]
    co_n, half = g_ref.shape[1], g_ref.shape[2]
    planes = cells // PLANE
    rows_w = 27 * co_n
    depth = 3 * co_n
    wide = base.shape[2]
    stages = len(orders[0])
    chunks = len(orders)
    co_me = lax.axis_index("co")
    ci_me = lax.axis_index("ci")

    def co_bit(bit):
        return lax.rem(co_me // (1 << bit), 2)

    def co_partner(bit):
        return co_me + (1 - 2 * co_bit(bit)) * (1 << bit)

    def ci_other(d):
        return lax.rem(ci_me + d, n_ci)

    load_w = pltpu.make_async_copy(w_hbm, w_ref.at[pl.ds(0, rows_w)], in_sem.at[0])
    load_f = pltpu.make_async_copy(f_hbm, f_ref, in_sem.at[1])
    load_g = pltpu.make_async_copy(g_hbm, g_ref.at[ci_me], in_sem.at[2])
    load_w.start()
    load_f.start()
    load_g.start()

    barrier = pltpu.get_barrier_semaphore()
    for bit in range(stages):
        pl.semaphore_signal(barrier, inc=1, device_id={"co": co_partner(bit)}, device_id_type=MESH)
    for d in range(1, n_ci):
        pl.semaphore_signal(barrier, inc=1, device_id={"ci": ci_other(d)}, device_id_type=MESH)
    pl.semaphore_wait(barrier, stages + n_ci - 1)

    g_copies = []
    for d in range(1, n_ci):
        copy = pltpu.make_async_remote_copy(
            src_ref=g_hbm, dst_ref=g_ref.at[ci_me],
            send_sem=gs_sem.at[d - 1], recv_sem=gr_sem.at[d - 1],
            device_id={"ci": ci_other(d)}, device_id_type=MESH,
        )
        copy.start()
        g_copies.append(copy)

    w_ref[rows_w:, :] = jnp.zeros((w_ref.shape[0] - rows_w, ci_n), w_ref.dtype)
    base[:, 0:PLANE, :] = jnp.zeros((3, PLANE, wide), base.dtype)
    base[:, PLANE + cells:, :] = jnp.zeros((3, PLANE, wide), base.dtype)
    def rows_of(owner):
        lane = lax.broadcasted_iota(jnp.int32, (LANES // NZ, NZ, wide), 2)
        k = lax.broadcasted_iota(jnp.int32, (LANES // NZ, NZ, wide), 1)
        first, last = (lane < co_n) & (k < NZ - 1), (lane >= 2 * co_n) & (lane < 3 * co_n) & (k > 0)
        middle = (lane >= co_n) & (lane < 2 * co_n)
        blank = jnp.zeros((LANES // PLANE, 1, NZ, wide), jnp.float32)
        for at in range(half // LANES):
            block = g_ref[owner, :, at * LANES:(at + 1) * LANES].astype(jnp.float32)
            turned = jnp.concatenate([block] * (wide // co_n), axis=0).T.reshape(LANES // NZ, NZ, wide)
            mixed = jnp.where(middle, turned, 0.0)
            mixed = jnp.where(first, pltpu.roll(turned, NZ - 1, 1), mixed)
            mixed = jnp.where(last, pltpu.roll(turned, 1, 1), mixed)
            mixed = mixed.reshape(LANES // PLANE, NY, NZ, wide)
            shifted = (
                jnp.concatenate([mixed[:, 1:], blank], axis=1),
                mixed,
                jnp.concatenate([blank, mixed[:, :-1]], axis=1),
            )
            rows = pl.ds(pl.multiple_of(PLANE + owner * half + at * LANES, PLANE), LANES)
            for b in range(3):
                base[b, rows, :] = shifted[b].reshape(LANES, wide).astype(base.dtype)

    load_g.wait()
    rows_of(ci_me)
    load_w.wait()
    load_f.wait()

    tile = 2 * LANES

    def response_tile(at):
        lane = lax.broadcasted_iota(jnp.int32, (co_n, tile), 1)
        k, j = lane & (NZ - 1), (lane // NZ) & (NY - 1)
        cols = f_ref[:, at * tile:(at + 1) * tile]
        for a in range(3):
            prod = jnp.dot(w_ref[a * 9 * co_n:(a + 1) * 9 * co_n, :], cols, preferred_element_type=jnp.float32)
            total = None
            for b in range(3):
                z = [prod[(3 * b + c) * co_n:(3 * b + c + 1) * co_n] for c in range(3)]
                part = z[1] + jnp.where(k > 0, pltpu.roll(z[0], 1, 1), 0.0)
                part = part + jnp.where(k < NZ - 1, pltpu.roll(z[2], tile - 1, 1), 0.0)
                if b == 0:
                    part = jnp.where(j > 0, pltpu.roll(part, NZ, 1), 0.0)
                if b == 2:
                    part = jnp.where(j < NY - 1, pltpu.roll(part, tile - NZ, 1), 0.0)
                total = part if total is None else total + part
            ysum[a, :, at * tile:(at + 1) * tile] = total

    tiles = cells // tile
    early = tiles // 2
    for at in range(early):
        response_tile(at)

    for d in range(1, n_ci):
        g_copies[d - 1].wait_recv()
        rows_of(lax.rem(ci_me + n_ci - d, n_ci))

    cols_w = min(2 * LANES, ci_n)
    group = 8
    per = cols_w // LANES

    def shares(h):
        for first in range(0, planes, group):
            total = None
            for b in range(3):
                starts = [(first + 2 - a) * PLANE for a in range(3)]
                tops = [(3 * a + b) * depth for a in range(3)]
                term = jnp.dot(
                    jnp.concatenate([base[b, start:start + group * PLANE, :] for start in starts], axis=1),
                    jnp.concatenate([w_ref[top:top + wide, h * cols_w:(h + 1) * cols_w] for top in tops], axis=0),
                    preferred_element_type=jnp.float32,
                )
                total = term if total is None else total + term
            for q in range(per):
                c = h * per + q
                for p in range(group):
                    acc[c, place(first + p, orders[c])] = total[
                        p * PLANE:(p + 1) * PLANE, q * LANES:(q + 1) * LANES
                    ]

    def where_at(c, s):
        spot = 0
        for n in range(s):
            spot = spot + co_bit(orders[c][n]) * (n_co >> (n + 1))
        return spot

    def halving(c, s):
        size = n_co >> (s + 1)
        bit = orders[c][s]
        return pltpu.make_async_remote_copy(
            src_ref=acc.at[c, pl.ds(where_at(c, s) + (1 - co_bit(bit)) * size, size)],
            dst_ref=recvs[s].at[c],
            send_sem=hs_sem.at[c * stages + s], recv_sem=hr_sem.at[c * stages + s],
            device_id={"co": co_partner(bit)}, device_id_type=MESH,
        )

    def begin(c, s):
        halving(c, s).start()

    def arrive(c, s):
        halving(c, s).wait_recv()
        size = n_co >> (s + 1)
        spot = pl.ds(where_at(c, s + 1), size)
        if s + 1 < stages:
            acc[c, spot] = acc[c, spot] + recvs[s][c]
        else:
            block = acc[c, where_at(c, s + 1)] + recvs[s][c, 0]
            ingrad_ref[:, c * LANES:(c + 1) * LANES] = block.astype(ingrad_ref.dtype)

    def step(c, s):
        arrive(c, s)
        if s + 1 < stages:
            begin(c, s + 1)

    halves = ci_n // cols_w
    for h in range(halves):
        shares(h)
        for q in range(per):
            begin(h * per + q, 0)
    lead = [0] + list(range(2, chunks))
    step(0, 0)
    if chunks > 1:
        step(1, 0)
    for at in range(early, tiles):
        response_tile(at)
    for c in lead[1:]:
        arrive(c, 0)
        if c == lead[1]:
            begin(c, 1)

    lane = lax.broadcasted_iota(jnp.int32, (co_n, cells), 1)
    whole = ysum[1] + jnp.where(lane >= PLANE, pltpu.roll(ysum[0], PLANE, 1), 0.0)
    whole = whole + jnp.where(lane < cells - PLANE, pltpu.roll(ysum[2], cells - PLANE, 1), 0.0)
    for n in range(n_ci):
        rpart[n] = whole[:, n * half:(n + 1) * half]
    r_copies = []
    for d in range(1, n_ci):
        copy = pltpu.make_async_remote_copy(
            src_ref=rpart.at[ci_other(d)], dst_ref=rrecv.at[d - 1],
            send_sem=rs_sem.at[d - 1], recv_sem=rr_sem.at[d - 1],
            device_id={"ci": ci_other(d)}, device_id_type=MESH,
        )
        copy.start()
        r_copies.append(copy)

    strip = 16
    lane = lax.broadcasted_iota(jnp.int32, (strip, cells), 1)
    k, j = lane & (NZ - 1), (lane // NZ) & (NY - 1)
    edge = jnp.zeros((strip, LANES), jnp.float32)

    def lay(c):
        for top in range(0, co_n, strip):
            v = jnp.concatenate([g_ref[n, top:top + strip, :] for n in range(n_ci)], axis=1).astype(jnp.float32)
            if c == 0:
                v = jnp.where(k < NZ - 1, pltpu.roll(v, cells - 1, 1), 0.0)
            if c == 2:
                v = jnp.where(k > 0, pltpu.roll(v, 1, 1), 0.0)
            for b in range(3):
                u = v
                if b == 0:
                    u = jnp.where(j < NY - 1, pltpu.roll(v, cells - NZ, 1), 0.0)
                if b == 2:
                    u = jnp.where(j > 0, pltpu.roll(v, NZ, 1), 0.0)
                rows = slice((3 * b + c) * co_n + top, (3 * b + c) * co_n + top + strip)
                u_mid[rows, :] = u.astype(u_mid.dtype)
                u_side[rows, :] = pltpu.roll(jnp.concatenate([u, edge], axis=1), PLANE, 1).astype(u_side.dtype)

    scale = float(cells) ** -0.5

    def weights(a, h):
        left = u_mid[...] if a == 1 else (u_side[:, 2 * PLANE:2 * PLANE + cells] if a == 0 else u_side[:, 0:cells])
        cols = slice(h * cols_w, (h + 1) * cols_w)
        prod = lax.dot_general(left, f_ref[cols, :], (((1,), (1,)), ((), ())), preferred_element_type=jnp.float32)
        fg_ref[a * 9 * co_n:(a + 1) * 9 * co_n, cols] = prod * scale

    work = [functools.partial(lay, c) for c in range(3)]
    work += [functools.partial(weights, a, h) for a in range(3) for h in range(halves)]

    def compute(count):
        for _ in range(min(count, len(work))):
            work.pop(0)()

    compute(1)
    open_at = {1: 1} if chunks > 1 else {}
    for turn, c in enumerate(lead):
        step(c, 1)
        if turn + 2 < len(lead):
            begin(lead[turn + 2], 1)
        for other in list(open_at):
            if open_at[other] < stages:
                step(other, open_at[other])
                open_at[other] += 1
            compute(1)
        open_at[c] = 2
        compute(1)
    while any(s < stages for s in open_at.values()):
        for other in open_at:
            if open_at[other] < stages:
                step(other, open_at[other])
                open_at[other] += 1
                compute(1)
    compute(len(work))

    mine = rpart[ci_me]
    for d in range(1, n_ci):
        r_copies[d - 1].wait_recv()
        mine = mine + rrecv[d - 1]
    resp_ref[...] = mine.astype(resp_ref.dtype)

    for c in range(chunks):
        for s in range(stages):
            halving(c, s).wait_send()
    for copy in g_copies + r_copies:
        copy.wait_send()


def hand_over(r_ref, i_ref, w_ref, r_out, i_out, w_out, sem):
    rows = w_ref.shape[0] // 27
    copies = [pltpu.make_async_copy(r_ref, r_out, sem.at[0]), pltpu.make_async_copy(i_ref, i_out, sem.at[1])]
    for t in range(27):
        part = pl.ds(t * rows, rows)
        copies.append(pltpu.make_async_copy(w_ref.at[part], w_out.at[part], sem.at[2 + t]))
    for copy in copies:
        copy.start()
    for copy in copies:
        copy.wait()


def body(n_co, n_ci, features, filter_bank, out_grad):
    ci_n, cells = features.shape
    co_n, half = out_grad.shape
    stages = n_co.bit_length() - 1
    chunks = ci_n // LANES
    near = tuple(range(stages))
    far = (0,) + tuple(range(2, stages)) + (1,)
    orders = tuple(far if c == 1 else near for c in range(chunks))
    wide = -(-3 * co_n // LANES) * LANES
    rows_w = 27 * co_n
    dma = pltpu.SemaphoreType.DMA
    other = max(n_ci - 1, 1)
    scratch = [
        pltpu.VMEM((ci_n, cells), jnp.bfloat16),
        pltpu.VMEM((rows_w + wide - 3 * co_n, ci_n), jnp.bfloat16),
        pltpu.VMEM((n_ci, co_n, half), jnp.bfloat16),
        pltpu.VMEM((3, cells + 2 * PLANE, wide), jnp.bfloat16),
        pltpu.VMEM((chunks, n_co, PLANE, LANES), jnp.float32),
        [pltpu.VMEM((chunks, n_co >> (s + 1), PLANE, LANES), jnp.float32) for s in range(stages)],
        pltpu.VMEM((3, co_n, cells), jnp.float32),
        pltpu.VMEM((n_ci, co_n, half), jnp.float32),
        pltpu.VMEM((other, co_n, half), jnp.float32),
        pltpu.VMEM((9 * co_n, cells), jnp.bfloat16),
        pltpu.VMEM((9 * co_n, cells + 2 * PLANE), jnp.bfloat16),
        dma((3,)), dma((other,)), dma((other,)), dma((other,)), dma((other,)),
        dma((chunks * stages,)), dma((chunks * stages,)),
    ]
    hbm = pl.BlockSpec(memory_space=pltpu.HBM)
    vmem = pl.BlockSpec(memory_space=pltpu.VMEM)
    shapes = (
        jax.ShapeDtypeStruct((co_n, half), jnp.bfloat16),
        jax.ShapeDtypeStruct((cells // n_co, ci_n), jnp.bfloat16),
        jax.ShapeDtypeStruct((rows_w, ci_n), jnp.float32),
    )
    results = pl.pallas_call(
        functools.partial(kernel, n_co, n_ci, orders),
        out_shape=shapes,
        in_specs=[hbm] * 3,
        out_specs=(vmem,) * 3,
        scratch_shapes=scratch,
        compiler_params=pltpu.CompilerParams(
            collective_id=0, has_side_effects=True, vmem_limit_bytes=32 * 1024 * 1024
        ),
        cost_estimate=pl.CostEstimate(
            flops=6 * rows_w * ci_n * cells, bytes_accessed=8 * rows_w * ci_n, transcendentals=0
        ),
    )(*[pltpu.with_memory_space_constraint(v, pltpu.HBM) for v in (features, filter_bank.reshape(rows_w, ci_n), out_grad)])
    response, in_grad, filter_grad = pl.pallas_call(
        hand_over,
        out_shape=shapes,
        in_specs=[vmem] * 3,
        out_specs=(hbm,) * 3,
        scratch_shapes=[dma((29,))],
        compiler_params=pltpu.CompilerParams(vmem_limit_bytes=8 * 1024 * 1024),
        cost_estimate=pl.CostEstimate(flops=0, bytes_accessed=8 * rows_w * ci_n, transcendentals=0),
    )(*[pltpu.with_memory_space_constraint(v, pltpu.VMEM) for v in results])
    return response, in_grad.T, filter_grad.reshape(27, co_n, ci_n)


def solution(mesh):
    placed = (P("ci", None), P(None, "co", "ci"), P("co", "ci"))
    return jax.shard_map(
        functools.partial(body, mesh.shape["co"], mesh.shape["ci"]),
        mesh=mesh,
        in_specs=placed,
        out_specs=(P("co", "ci"), P("ci", "co"), P(None, "co", "ci")),
        check_vma=False,
    )
```

```python
import functools

import jax
import jax.numpy as jnp
from jax import lax
from jax.experimental import pallas as pl
from jax.experimental.pallas import tpu as pltpu
from jax.sharding import PartitionSpec as P

NY = 8
NZ = 8
PLANE = NY * NZ
LANES = 128
MESH = pl.DeviceIdType.MESH


def place(plane, order):
    spot = 0
    for bit in order:
        spot = spot * 2 + (plane >> bit) % 2
    return spot


def kernel(
    n_co, n_ci, orders,
    f_hbm, w_hbm, g_hbm,
    resp_ref, ingrad_ref, fg_ref,
    f_ref, w_ref, g_ref, base, acc, recvs, ysum, rpart, rrecv, u_mid, u_side,
    in_sem, gs_sem, gr_sem, rs_sem, rr_sem, hs_sem, hr_sem,
):
    cells = f_ref.shape[1]
    ci_n = f_ref.shape[0]
    co_n, half = g_ref.shape[1], g_ref.shape[2]
    planes = cells // PLANE
    rows_w = 27 * co_n
    depth = 3 * co_n
    wide = base.shape[2]
    stages = len(orders[0])
    chunks = len(orders)
    part = acc.shape[2]
    pieces = PLANE // part
    co_me = lax.axis_index("co")
    ci_me = lax.axis_index("ci")

    def co_bit(bit):
        return lax.rem(co_me // (1 << bit), 2)

    def co_partner(bit):
        return co_me + (1 - 2 * co_bit(bit)) * (1 << bit)

    def ci_other(d):
        return lax.rem(ci_me + d, n_ci)

    load_w = pltpu.make_async_copy(w_hbm, w_ref.at[pl.ds(0, rows_w)], in_sem.at[0])
    load_f = pltpu.make_async_copy(f_hbm, f_ref, in_sem.at[1])
    load_g = pltpu.make_async_copy(g_hbm, g_ref.at[ci_me], in_sem.at[2])
    load_w.start()
    load_f.start()
    load_g.start()

    barrier = pltpu.get_barrier_semaphore()
    for bit in range(stages):
        pl.semaphore_signal(barrier, inc=1, device_id={"co": co_partner(bit)}, device_id_type=MESH)
    for d in range(1, n_ci):
        pl.semaphore_signal(barrier, inc=1, device_id={"ci": ci_other(d)}, device_id_type=MESH)
    pl.semaphore_wait(barrier, stages + n_ci - 1)

    g_copies = []
    for d in range(1, n_ci):
        copy = pltpu.make_async_remote_copy(
            src_ref=g_hbm, dst_ref=g_ref.at[ci_me],
            send_sem=gs_sem.at[d - 1], recv_sem=gr_sem.at[d - 1],
            device_id={"ci": ci_other(d)}, device_id_type=MESH,
        )
        copy.start()
        g_copies.append(copy)

    w_ref[rows_w:, :] = jnp.zeros((w_ref.shape[0] - rows_w, ci_n), w_ref.dtype)
    base[:, 0:PLANE, :] = jnp.zeros((3, PLANE, wide), base.dtype)
    base[:, PLANE + cells:, :] = jnp.zeros((3, PLANE, wide), base.dtype)
    def rows_of(owner):
        lane = lax.broadcasted_iota(jnp.int32, (LANES // NZ, NZ, wide), 2)
        k = lax.broadcasted_iota(jnp.int32, (LANES // NZ, NZ, wide), 1)
        first, last = (lane < co_n) & (k < NZ - 1), (lane >= 2 * co_n) & (lane < 3 * co_n) & (k > 0)
        middle = (lane >= co_n) & (lane < 2 * co_n)
        blank = jnp.zeros((LANES // PLANE, 1, NZ, wide), jnp.float32)
        for at in range(half // LANES):
            block = g_ref[owner, :, at * LANES:(at + 1) * LANES].astype(jnp.float32)
            turned = jnp.concatenate([block] * (wide // co_n), axis=0).T.reshape(LANES // NZ, NZ, wide)
            mixed = jnp.where(middle, turned, 0.0)
            mixed = jnp.where(first, pltpu.roll(turned, NZ - 1, 1), mixed)
            mixed = jnp.where(last, pltpu.roll(turned, 1, 1), mixed)
            mixed = mixed.reshape(LANES // PLANE, NY, NZ, wide)
            shifted = (
                jnp.concatenate([mixed[:, 1:], blank], axis=1),
                mixed,
                jnp.concatenate([blank, mixed[:, :-1]], axis=1),
            )
            rows = pl.ds(pl.multiple_of(PLANE + owner * half + at * LANES, PLANE), LANES)
            for b in range(3):
                base[b, rows, :] = shifted[b].reshape(LANES, wide).astype(base.dtype)

    load_g.wait()
    rows_of(ci_me)
    load_w.wait()
    load_f.wait()

    tile = 2 * LANES

    def response_tile(at):
        lane = lax.broadcasted_iota(jnp.int32, (co_n, tile), 1)
        k, j = lane & (NZ - 1), (lane // NZ) & (NY - 1)
        cols = f_ref[:, at * tile:(at + 1) * tile]
        for a in range(3):
            prod = jnp.dot(w_ref[a * 9 * co_n:(a + 1) * 9 * co_n, :], cols, preferred_element_type=jnp.float32)
            total = None
            for b in range(3):
                z = [prod[(3 * b + c) * co_n:(3 * b + c + 1) * co_n] for c in range(3)]
                part = z[1] + jnp.where(k > 0, pltpu.roll(z[0], 1, 1), 0.0)
                part = part + jnp.where(k < NZ - 1, pltpu.roll(z[2], tile - 1, 1), 0.0)
                if b == 0:
                    part = jnp.where(j > 0, pltpu.roll(part, NZ, 1), 0.0)
                if b == 2:
                    part = jnp.where(j < NY - 1, pltpu.roll(part, tile - NZ, 1), 0.0)
                total = part if total is None else total + part
            ysum[a, :, at * tile:(at + 1) * tile] = total

    tiles = cells // tile

    for d in range(1, n_ci):
        g_copies[d - 1].wait_recv()
        rows_of(lax.rem(ci_me + n_ci - d, n_ci))

    cols_w = min(2 * LANES, ci_n)
    group = 8
    per = cols_w // LANES

    def shares(h):
        for first in range(0, planes, group):
            total = None
            for b in range(3):
                starts = [(first + 2 - a) * PLANE for a in range(3)]
                tops = [(3 * a + b) * depth for a in range(3)]
                term = jnp.dot(
                    jnp.concatenate([base[b, start:start + group * PLANE, :] for start in starts], axis=1),
                    jnp.concatenate([w_ref[top:top + wide, h * cols_w:(h + 1) * cols_w] for top in tops], axis=0),
                    preferred_element_type=jnp.float32,
                )
                total = term if total is None else total + term
            for q in range(per):
                for r in range(pieces):
                    c = (h * per + q) * pieces + r
                    for p in range(group):
                        top = p * PLANE + r * part
                        acc[c, place(first + p, orders[c])] = total[top:top + part, q * LANES:(q + 1) * LANES]

    def where_at(c, s):
        spot = 0
        for n in range(s):
            spot = spot + co_bit(orders[c][n]) * (n_co >> (n + 1))
        return spot

    def halving(c, s):
        size = n_co >> (s + 1)
        bit = orders[c][s]
        return pltpu.make_async_remote_copy(
            src_ref=acc.at[c, pl.ds(where_at(c, s) + (1 - co_bit(bit)) * size, size)],
            dst_ref=recvs[s].at[c],
            send_sem=hs_sem.at[c * stages + s], recv_sem=hr_sem.at[c * stages + s],
            device_id={"co": co_partner(bit)}, device_id_type=MESH,
        )

    def begin(c, s):
        halving(c, s).start()

    def arrive(c, s):
        halving(c, s).wait_recv()
        size = n_co >> (s + 1)
        spot = pl.ds(where_at(c, s + 1), size)
        if s + 1 < stages:
            acc[c, spot] = acc[c, spot] + recvs[s][c]
        else:
            block = acc[c, where_at(c, s + 1)] + recvs[s][c, 0]
            q, r = c // pieces, c % pieces
            ingrad_ref[r * part:(r + 1) * part, q * LANES:(q + 1) * LANES] = block.astype(ingrad_ref.dtype)

    def step(c, s):
        arrive(c, s)
        if s + 1 < stages:
            begin(c, s + 1)

    halves = ci_n // cols_w
    lead = [c for c in range(chunks) if orders[c][1] == 1]
    side = [c for c in range(chunks) if orders[c][1] != 1]
    flying = 3
    for h in range(halves):
        shares(h)
        for c in range(h * per * pieces, (h + 1) * per * pieces):
            begin(c, 0)
    for c in lead[:flying - 1] + side:
        step(c, 0)
    response_tile(0)
    for c in lead[flying - 1:flying]:
        step(c, 0)
    for at in range(1, tiles):
        response_tile(at)
    for c in lead[flying:]:
        arrive(c, 0)

    lane = lax.broadcasted_iota(jnp.int32, (co_n, cells), 1)
    whole = ysum[1] + jnp.where(lane >= PLANE, pltpu.roll(ysum[0], PLANE, 1), 0.0)
    whole = whole + jnp.where(lane < cells - PLANE, pltpu.roll(ysum[2], cells - PLANE, 1), 0.0)
    for n in range(n_ci):
        rpart[n] = whole[:, n * half:(n + 1) * half]
    r_copies = []
    for d in range(1, n_ci):
        copy = pltpu.make_async_remote_copy(
            src_ref=rpart.at[ci_other(d)], dst_ref=rrecv.at[d - 1],
            send_sem=rs_sem.at[d - 1], recv_sem=rr_sem.at[d - 1],
            device_id={"ci": ci_other(d)}, device_id_type=MESH,
        )
        copy.start()
        r_copies.append(copy)

    strip = 16
    lane = lax.broadcasted_iota(jnp.int32, (strip, cells), 1)
    k, j = lane & (NZ - 1), (lane // NZ) & (NY - 1)
    edge = jnp.zeros((strip, LANES), jnp.float32)

    def lay(c):
        for top in range(0, co_n, strip):
            v = jnp.concatenate([g_ref[n, top:top + strip, :] for n in range(n_ci)], axis=1).astype(jnp.float32)
            if c == 0:
                v = jnp.where(k < NZ - 1, pltpu.roll(v, cells - 1, 1), 0.0)
            if c == 2:
                v = jnp.where(k > 0, pltpu.roll(v, 1, 1), 0.0)
            for b in range(3):
                u = v
                if b == 0:
                    u = jnp.where(j < NY - 1, pltpu.roll(v, cells - NZ, 1), 0.0)
                if b == 2:
                    u = jnp.where(j > 0, pltpu.roll(v, NZ, 1), 0.0)
                rows = slice((3 * b + c) * co_n + top, (3 * b + c) * co_n + top + strip)
                u_mid[rows, :] = u.astype(u_mid.dtype)
                u_side[rows, :] = pltpu.roll(jnp.concatenate([u, edge], axis=1), PLANE, 1).astype(u_side.dtype)

    scale = float(cells) ** -0.5

    def weights(a, h):
        left = u_mid[...] if a == 1 else (u_side[:, 2 * PLANE:2 * PLANE + cells] if a == 0 else u_side[:, 0:cells])
        cols = slice(h * cols_w, (h + 1) * cols_w)
        prod = lax.dot_general(left, f_ref[cols, :], (((1,), (1,)), ((), ())), preferred_element_type=jnp.float32)
        fg_ref[a * 9 * co_n:(a + 1) * 9 * co_n, cols] = prod * scale

    work = [functools.partial(lay, c) for c in range(3)]
    work += [functools.partial(weights, a, h) for a in range(3) for h in range(halves)]

    def compute(count):
        for _ in range(min(count, len(work))):
            work.pop(0)()

    compute(1)
    reached = {c: 1 for c in side}

    def advance():
        for c in list(reached):
            if reached[c] < stages:
                step(c, reached[c])
                reached[c] += 1

    for turn, c in enumerate(lead):
        step(c, 1)
        if turn + flying < len(lead):
            begin(lead[turn + flying], 1)
        compute(1)
        advance()
        reached[c] = 2
        compute(1)
    while any(s < stages for s in reached.values()):
        advance()
    compute(len(work))

    mine = rpart[ci_me]
    for d in range(1, n_ci):
        r_copies[d - 1].wait_recv()
        mine = mine + rrecv[d - 1]
    resp_ref[...] = mine.astype(resp_ref.dtype)

    for c in range(chunks):
        for s in range(stages):
            halving(c, s).wait_send()
    for copy in g_copies + r_copies:
        copy.wait_send()


def hand_over(r_ref, i_ref, w_ref, r_out, i_out, w_out, sem):
    rows = w_ref.shape[0] // 27
    copies = [pltpu.make_async_copy(r_ref, r_out, sem.at[0]), pltpu.make_async_copy(i_ref, i_out, sem.at[1])]
    for t in range(27):
        part = pl.ds(t * rows, rows)
        copies.append(pltpu.make_async_copy(w_ref.at[part], w_out.at[part], sem.at[2 + t]))
    for copy in copies:
        copy.start()
    for copy in copies:
        copy.wait()


def body(n_co, n_ci, features, filter_bank, out_grad):
    ci_n, cells = features.shape
    co_n, half = out_grad.shape
    stages = n_co.bit_length() - 1
    pieces = 2
    chunks = ci_n // LANES * pieces
    near = tuple(range(stages))
    far = (0,) + tuple(range(2, stages)) + (1,)
    orders = tuple(far if c // pieces == 1 else near for c in range(chunks))
    wide = -(-3 * co_n // LANES) * LANES
    rows_w = 27 * co_n
    dma = pltpu.SemaphoreType.DMA
    other = max(n_ci - 1, 1)
    scratch = [
        pltpu.VMEM((ci_n, cells), jnp.bfloat16),
        pltpu.VMEM((rows_w + wide - 3 * co_n, ci_n), jnp.bfloat16),
        pltpu.VMEM((n_ci, co_n, half), jnp.bfloat16),
        pltpu.VMEM((3, cells + 2 * PLANE, wide), jnp.bfloat16),
        pltpu.VMEM((chunks, n_co, PLANE // pieces, LANES), jnp.float32),
        [pltpu.VMEM((chunks, n_co >> (s + 1), PLANE // pieces, LANES), jnp.float32) for s in range(stages)],
        pltpu.VMEM((3, co_n, cells), jnp.float32),
        pltpu.VMEM((n_ci, co_n, half), jnp.float32),
        pltpu.VMEM((other, co_n, half), jnp.float32),
        pltpu.VMEM((9 * co_n, cells), jnp.bfloat16),
        pltpu.VMEM((9 * co_n, cells + 2 * PLANE), jnp.bfloat16),
        dma((3,)), dma((other,)), dma((other,)), dma((other,)), dma((other,)),
        dma((chunks * stages,)), dma((chunks * stages,)),
    ]
    hbm = pl.BlockSpec(memory_space=pltpu.HBM)
    vmem = pl.BlockSpec(memory_space=pltpu.VMEM)
    shapes = (
        jax.ShapeDtypeStruct((co_n, half), jnp.bfloat16),
        jax.ShapeDtypeStruct((cells // n_co, ci_n), jnp.bfloat16),
        jax.ShapeDtypeStruct((rows_w, ci_n), jnp.float32),
    )
    results = pl.pallas_call(
        functools.partial(kernel, n_co, n_ci, orders),
        out_shape=shapes,
        in_specs=[hbm] * 3,
        out_specs=(vmem,) * 3,
        scratch_shapes=scratch,
        compiler_params=pltpu.CompilerParams(
            collective_id=0, has_side_effects=True, vmem_limit_bytes=32 * 1024 * 1024
        ),
        cost_estimate=pl.CostEstimate(
            flops=6 * rows_w * ci_n * cells, bytes_accessed=8 * rows_w * ci_n, transcendentals=0
        ),
    )(*[pltpu.with_memory_space_constraint(v, pltpu.HBM) for v in (features, filter_bank.reshape(rows_w, ci_n), out_grad)])
    response, in_grad, filter_grad = pl.pallas_call(
        hand_over,
        out_shape=shapes,
        in_specs=[vmem] * 3,
        out_specs=(hbm,) * 3,
        scratch_shapes=[dma((29,))],
        compiler_params=pltpu.CompilerParams(vmem_limit_bytes=8 * 1024 * 1024),
        cost_estimate=pl.CostEstimate(flops=0, bytes_accessed=8 * rows_w * ci_n, transcendentals=0),
    )(*[pltpu.with_memory_space_constraint(v, pltpu.VMEM) for v in results])
    return response, in_grad.T, filter_grad.reshape(27, co_n, ci_n)


def solution(mesh):
    placed = (P("ci", None), P(None, "co", "ci"), P("co", "ci"))
    return jax.shard_map(
        functools.partial(body, mesh.shape["co"], mesh.shape["ci"]),
        mesh=mesh,
        in_specs=placed,
        out_specs=(P("co", "ci"), P("ci", "co"), P(None, "co", "ci")),
        check_vma=False,
    )
```

```python
import functools

import jax
import jax.numpy as jnp
from jax import lax
from jax.experimental import pallas as pl
from jax.experimental.pallas import tpu as pltpu
from jax.sharding import PartitionSpec as P

NY = 8
NZ = 8
PLANE = NY * NZ
LANES = 128
MESH = pl.DeviceIdType.MESH


def place(plane, order):
    spot = 0
    for bit in order:
        spot = spot * 2 + (plane >> bit) % 2
    return spot


def kernel(
    n_co, n_ci, orders,
    f_hbm, w_hbm, g_hbm,
    resp_ref, ingrad_ref, fg_ref,
    f_ref, w_ref, g_ref, base, acc, recvs, ysum, rpart, rrecv, u_mid, u_side,
    in_sem, gs_sem, gr_sem, rs_sem, rr_sem, hs_sem, hr_sem,
):
    cells = f_ref.shape[1]
    ci_n = f_ref.shape[0]
    co_n, half = g_ref.shape[1], g_ref.shape[2]
    planes = cells // PLANE
    rows_w = 27 * co_n
    depth = 3 * co_n
    wide = base.shape[2]
    stages = len(orders[0])
    chunks = len(orders)
    cut = acc.shape[3]
    co_me = lax.axis_index("co")
    ci_me = lax.axis_index("ci")

    def co_bit(bit):
        return lax.rem(co_me // (1 << bit), 2)

    def co_partner(bit):
        return co_me + (1 - 2 * co_bit(bit)) * (1 << bit)

    def ci_other(d):
        return lax.rem(ci_me + d, n_ci)

    load_w = pltpu.make_async_copy(w_hbm, w_ref.at[pl.ds(0, rows_w)], in_sem.at[0])
    load_f = pltpu.make_async_copy(f_hbm, f_ref, in_sem.at[1])
    load_g = pltpu.make_async_copy(g_hbm, g_ref.at[ci_me], in_sem.at[2])
    load_w.start()
    load_f.start()
    load_g.start()

    barrier = pltpu.get_barrier_semaphore()
    for bit in range(stages):
        pl.semaphore_signal(barrier, inc=1, device_id={"co": co_partner(bit)}, device_id_type=MESH)
    for d in range(1, n_ci):
        pl.semaphore_signal(barrier, inc=1, device_id={"ci": ci_other(d)}, device_id_type=MESH)
    pl.semaphore_wait(barrier, stages + n_ci - 1)

    g_copies = []
    for d in range(1, n_ci):
        copy = pltpu.make_async_remote_copy(
            src_ref=g_hbm, dst_ref=g_ref.at[ci_me],
            send_sem=gs_sem.at[d - 1], recv_sem=gr_sem.at[d - 1],
            device_id={"ci": ci_other(d)}, device_id_type=MESH,
        )
        copy.start()
        g_copies.append(copy)

    w_ref[rows_w:, :] = jnp.zeros((w_ref.shape[0] - rows_w, ci_n), w_ref.dtype)
    base[:, 0:PLANE, :] = jnp.zeros((3, PLANE, wide), base.dtype)
    base[:, PLANE + cells:, :] = jnp.zeros((3, PLANE, wide), base.dtype)
    def rows_of(owner):
        lane = lax.broadcasted_iota(jnp.int32, (LANES // NZ, NZ, wide), 2)
        k = lax.broadcasted_iota(jnp.int32, (LANES // NZ, NZ, wide), 1)
        first, last = (lane < co_n) & (k < NZ - 1), (lane >= 2 * co_n) & (lane < 3 * co_n) & (k > 0)
        middle = (lane >= co_n) & (lane < 2 * co_n)
        blank = jnp.zeros((LANES // PLANE, 1, NZ, wide), jnp.float32)
        for at in range(half // LANES):
            block = g_ref[owner, :, at * LANES:(at + 1) * LANES].astype(jnp.float32)
            turned = jnp.concatenate([block] * (wide // co_n), axis=0).T.reshape(LANES // NZ, NZ, wide)
            mixed = jnp.where(middle, turned, 0.0)
            mixed = jnp.where(first, pltpu.roll(turned, NZ - 1, 1), mixed)
            mixed = jnp.where(last, pltpu.roll(turned, 1, 1), mixed)
            mixed = mixed.reshape(LANES // PLANE, NY, NZ, wide)
            shifted = (
                jnp.concatenate([mixed[:, 1:], blank], axis=1),
                mixed,
                jnp.concatenate([blank, mixed[:, :-1]], axis=1),
            )
            rows = pl.ds(pl.multiple_of(PLANE + owner * half + at * LANES, PLANE), LANES)
            for b in range(3):
                base[b, rows, :] = shifted[b].reshape(LANES, wide).astype(base.dtype)

    load_g.wait()
    rows_of(ci_me)
    load_w.wait()
    load_f.wait()

    tile = 2 * LANES

    def response_tile(at):
        lane = lax.broadcasted_iota(jnp.int32, (co_n, tile), 1)
        k, j = lane & (NZ - 1), (lane // NZ) & (NY - 1)
        cols = f_ref[:, at * tile:(at + 1) * tile]
        for a in range(3):
            prod = jnp.dot(w_ref[a * 9 * co_n:(a + 1) * 9 * co_n, :], cols, preferred_element_type=jnp.float32)
            total = None
            for b in range(3):
                z = [prod[(3 * b + c) * co_n:(3 * b + c + 1) * co_n] for c in range(3)]
                part = z[1] + jnp.where(k > 0, pltpu.roll(z[0], 1, 1), 0.0)
                part = part + jnp.where(k < NZ - 1, pltpu.roll(z[2], tile - 1, 1), 0.0)
                if b == 0:
                    part = jnp.where(j > 0, pltpu.roll(part, NZ, 1), 0.0)
                if b == 2:
                    part = jnp.where(j < NY - 1, pltpu.roll(part, tile - NZ, 1), 0.0)
                total = part if total is None else total + part
            ysum[a, :, at * tile:(at + 1) * tile] = total

    tiles = cells // tile
    early = tiles // 2
    for at in range(early):
        response_tile(at)

    for d in range(1, n_ci):
        g_copies[d - 1].wait_recv()
        rows_of(lax.rem(ci_me + n_ci - d, n_ci))

    cols_w = min(2 * LANES, ci_n)
    group = 8
    per = cols_w // cut

    def shares(h):
        for first in range(0, planes, group):
            total = None
            for b in range(3):
                starts = [(first + 2 - a) * PLANE for a in range(3)]
                tops = [(3 * a + b) * depth for a in range(3)]
                term = jnp.dot(
                    jnp.concatenate([base[b, start:start + group * PLANE, :] for start in starts], axis=1),
                    jnp.concatenate([w_ref[top:top + wide, h * cols_w:(h + 1) * cols_w] for top in tops], axis=0),
                    preferred_element_type=jnp.float32,
                )
                total = term if total is None else total + term
            for q in range(per):
                c = h * per + q
                for p in range(group):
                    acc[c, place(first + p, orders[c])] = total[
                        p * PLANE:(p + 1) * PLANE, q * cut:(q + 1) * cut
                    ]

    def where_at(c, s):
        spot = 0
        for n in range(s):
            spot = spot + co_bit(orders[c][n]) * (n_co >> (n + 1))
        return spot

    def halving(c, s):
        size = n_co >> (s + 1)
        bit = orders[c][s]
        return pltpu.make_async_remote_copy(
            src_ref=acc.at[c, pl.ds(where_at(c, s) + (1 - co_bit(bit)) * size, size)],
            dst_ref=recvs[s].at[c],
            send_sem=hs_sem.at[c * stages + s], recv_sem=hr_sem.at[c * stages + s],
            device_id={"co": co_partner(bit)}, device_id_type=MESH,
        )

    def begin(c, s):
        halving(c, s).start()

    def arrive(c, s):
        halving(c, s).wait_recv()
        size = n_co >> (s + 1)
        spot = pl.ds(where_at(c, s + 1), size)
        if s + 1 < stages:
            acc[c, spot] = acc[c, spot] + recvs[s][c]
        else:
            block = acc[c, where_at(c, s + 1)] + recvs[s][c, 0]
            ingrad_ref[:, c * cut:(c + 1) * cut] = block.astype(ingrad_ref.dtype)

    def step(c, s):
        arrive(c, s)
        if s + 1 < stages:
            begin(c, s + 1)

    halves = ci_n // cols_w
    for h in range(halves):
        shares(h)
        for q in range(per):
            begin(h * per + q, 0)
    lead = [0] + list(range(2, chunks))
    step(0, 0)
    if chunks > 1:
        step(1, 0)
    for at in range(early, tiles):
        response_tile(at)
    for c in lead[1:]:
        arrive(c, 0)
        if c in lead[1:2]:
            begin(c, 1)

    lane = lax.broadcasted_iota(jnp.int32, (co_n, cells), 1)
    whole = ysum[1] + jnp.where(lane >= PLANE, pltpu.roll(ysum[0], PLANE, 1), 0.0)
    whole = whole + jnp.where(lane < cells - PLANE, pltpu.roll(ysum[2], cells - PLANE, 1), 0.0)
    for n in range(n_ci):
        rpart[n] = whole[:, n * half:(n + 1) * half]
    r_copies = []
    for d in range(1, n_ci):
        copy = pltpu.make_async_remote_copy(
            src_ref=rpart.at[ci_other(d)], dst_ref=rrecv.at[d - 1],
            send_sem=rs_sem.at[d - 1], recv_sem=rr_sem.at[d - 1],
            device_id={"ci": ci_other(d)}, device_id_type=MESH,
        )
        copy.start()
        r_copies.append(copy)

    strip = 16
    lane = lax.broadcasted_iota(jnp.int32, (strip, cells), 1)
    k, j = lane & (NZ - 1), (lane // NZ) & (NY - 1)
    edge = jnp.zeros((strip, LANES), jnp.float32)

    def lay(c):
        for top in range(0, co_n, strip):
            v = jnp.concatenate([g_ref[n, top:top + strip, :] for n in range(n_ci)], axis=1).astype(jnp.float32)
            if c == 0:
                v = jnp.where(k < NZ - 1, pltpu.roll(v, cells - 1, 1), 0.0)
            if c == 2:
                v = jnp.where(k > 0, pltpu.roll(v, 1, 1), 0.0)
            for b in range(3):
                u = v
                if b == 0:
                    u = jnp.where(j < NY - 1, pltpu.roll(v, cells - NZ, 1), 0.0)
                if b == 2:
                    u = jnp.where(j > 0, pltpu.roll(v, NZ, 1), 0.0)
                rows = slice((3 * b + c) * co_n + top, (3 * b + c) * co_n + top + strip)
                u_mid[rows, :] = u.astype(u_mid.dtype)
                u_side[rows, :] = pltpu.roll(jnp.concatenate([u, edge], axis=1), PLANE, 1).astype(u_side.dtype)

    scale = float(cells) ** -0.5

    def weights(a, h):
        left = u_mid[...] if a == 1 else (u_side[:, 2 * PLANE:2 * PLANE + cells] if a == 0 else u_side[:, 0:cells])
        cols = slice(h * cols_w, (h + 1) * cols_w)
        prod = lax.dot_general(left, f_ref[cols, :], (((1,), (1,)), ((), ())), preferred_element_type=jnp.float32)
        fg_ref[a * 9 * co_n:(a + 1) * 9 * co_n, cols] = prod * scale

    work = [functools.partial(lay, c) for c in range(3)]
    work += [functools.partial(weights, a, h) for a in range(3) for h in range(halves)]

    def compute(count):
        for _ in range(min(count, len(work))):
            work.pop(0)()

    compute(1)
    open_at = {1: 1} if chunks > 1 else {}
    for turn, c in enumerate(lead):
        step(c, 1)
        if turn + 2 < len(lead):
            begin(lead[turn + 2], 1)
        for other in list(open_at):
            if open_at[other] < stages:
                step(other, open_at[other])
                open_at[other] += 1
            compute(1)
        open_at[c] = 2
        compute(1)
    while any(s < stages for s in open_at.values()):
        for other in open_at:
            if open_at[other] < stages:
                step(other, open_at[other])
                open_at[other] += 1
                compute(1)
    compute(len(work))

    mine = rpart[ci_me]
    for d in range(1, n_ci):
        r_copies[d - 1].wait_recv()
        mine = mine + rrecv[d - 1]
    resp_ref[...] = mine.astype(resp_ref.dtype)

    for c in range(chunks):
        for s in range(stages):
            halving(c, s).wait_send()
    for copy in g_copies + r_copies:
        copy.wait_send()


def hand_over(r_ref, i_ref, w_ref, r_out, i_out, w_out, sem):
    rows = w_ref.shape[0] // 27
    copies = [pltpu.make_async_copy(r_ref, r_out, sem.at[0]), pltpu.make_async_copy(i_ref, i_out, sem.at[1])]
    for t in range(27):
        part = pl.ds(t * rows, rows)
        copies.append(pltpu.make_async_copy(w_ref.at[part], w_out.at[part], sem.at[2 + t]))
    for copy in copies:
        copy.start()
    for copy in copies:
        copy.wait()


def body(n_co, n_ci, features, filter_bank, out_grad):
    ci_n, cells = features.shape
    co_n, half = out_grad.shape
    stages = n_co.bit_length() - 1
    cut = min(2 * LANES, ci_n)
    chunks = ci_n // cut
    near = tuple(range(stages))
    far = (0,) + tuple(range(2, stages)) + (1,)
    orders = tuple(far if c == 1 else near for c in range(chunks))
    wide = -(-3 * co_n // LANES) * LANES
    rows_w = 27 * co_n
    dma = pltpu.SemaphoreType.DMA
    other = max(n_ci - 1, 1)
    scratch = [
        pltpu.VMEM((ci_n, cells), jnp.bfloat16),
        pltpu.VMEM((rows_w + wide - 3 * co_n, ci_n), jnp.bfloat16),
        pltpu.VMEM((n_ci, co_n, half), jnp.bfloat16),
        pltpu.VMEM((3, cells + 2 * PLANE, wide), jnp.bfloat16),
        pltpu.VMEM((chunks, n_co, PLANE, cut), jnp.float32),
        [pltpu.VMEM((chunks, n_co >> (s + 1), PLANE, cut), jnp.float32) for s in range(stages)],
        pltpu.VMEM((3, co_n, cells), jnp.float32),
        pltpu.VMEM((n_ci, co_n, half), jnp.float32),
        pltpu.VMEM((other, co_n, half), jnp.float32),
        pltpu.VMEM((9 * co_n, cells), jnp.bfloat16),
        pltpu.VMEM((9 * co_n, cells + 2 * PLANE), jnp.bfloat16),
        dma((3,)), dma((other,)), dma((other,)), dma((other,)), dma((other,)),
        dma((chunks * stages,)), dma((chunks * stages,)),
    ]
    hbm = pl.BlockSpec(memory_space=pltpu.HBM)
    vmem = pl.BlockSpec(memory_space=pltpu.VMEM)
    shapes = (
        jax.ShapeDtypeStruct((co_n, half), jnp.bfloat16),
        jax.ShapeDtypeStruct((cells // n_co, ci_n), jnp.bfloat16),
        jax.ShapeDtypeStruct((rows_w, ci_n), jnp.float32),
    )
    results = pl.pallas_call(
        functools.partial(kernel, n_co, n_ci, orders),
        out_shape=shapes,
        in_specs=[hbm] * 3,
        out_specs=(vmem,) * 3,
        scratch_shapes=scratch,
        compiler_params=pltpu.CompilerParams(
            collective_id=0, has_side_effects=True, vmem_limit_bytes=32 * 1024 * 1024
        ),
        cost_estimate=pl.CostEstimate(
            flops=6 * rows_w * ci_n * cells, bytes_accessed=8 * rows_w * ci_n, transcendentals=0
        ),
    )(*[pltpu.with_memory_space_constraint(v, pltpu.HBM) for v in (features, filter_bank.reshape(rows_w, ci_n), out_grad)])
    response, in_grad, filter_grad = pl.pallas_call(
        hand_over,
        out_shape=shapes,
        in_specs=[vmem] * 3,
        out_specs=(hbm,) * 3,
        scratch_shapes=[dma((29,))],
        compiler_params=pltpu.CompilerParams(vmem_limit_bytes=8 * 1024 * 1024),
        cost_estimate=pl.CostEstimate(flops=0, bytes_accessed=8 * rows_w * ci_n, transcendentals=0),
    )(*[pltpu.with_memory_space_constraint(v, pltpu.VMEM) for v in results])
    return response, in_grad.T, filter_grad.reshape(27, co_n, ci_n)


def solution(mesh):
    placed = (P("ci", None), P(None, "co", "ci"), P("co", "ci"))
    return jax.shard_map(
        functools.partial(body, mesh.shape["co"], mesh.shape["ci"]),
        mesh=mesh,
        in_specs=placed,
        out_specs=(P("co", "ci"), P("ci", "co"), P(None, "co", "ci")),
        check_vma=False,
    )
```
